32 devices in a mesh: samples: 2 (over y), theta: 4 (over z), band: 2 (over x), row: 2 (over core).
Axes of the slice: x: 2, y: 2, z: 4, core: 2. Of those that a mesh axis runs over, the one named last changes fastest.
Arguments:
- adjoint: float32 [4, 5, 64, 32, 128], P(('samples', 'row'), None, 'theta', 'band'), parts along dimension 0, may hold values from -6 to 6
- objective_grad: float32 [4, 5, 64, 32, 128], P(('samples', 'row'), None, 'theta', 'band'), parts along dimension 0, may hold values from -12 to 12
- face_coef: float32 [4, 3, 64, 32, 128], P(('samples', 'row'), None, 'theta', 'band'), parts along dimension 0, may hold values from 0.5 to 2
- source: float32 [4, 64, 32, 128], P(('samples', 'row'), 'theta', 'band'), parts along dimension 0, may hold values from 0.5 to 4
- flux_jac: float32 [2, 3, 2, 5, 5], P('row'), may hold values from -2.5 to 2.5
- mix_weight: float32 [4, 64, 32], P(('samples', 'row'), 'theta', 'band'), parts along dimension 0, may hold values from 0.25 to 1
- mix_map: int32 [4, 32], P(('samples', 'row'), 'band'), parts along dimension 0, may hold values from 0 to 31
- mix_jac: float32 [2, 5, 5], P('row'), may hold values from -2.5 to 2.5
- surf_weight: float32 [4, 5, 4, 32, 128], P(('samples', 'row'), None, 'theta', 'band'), parts along dimension 0, may hold values from -1.5 to 1.5
- patch_mode: int32 [4, 4, 32], P(('samples', 'row'), 'theta', 'band'), parts along dimension 0, may hold values from 0 to 31
Outputs:
- adjoint_out: float32 [4, 5, 64, 32, 128], P(('samples', 'row'), None, 'theta', 'band'), parts along dimension 0
- sensitivity: float32 [64, 128], P(('samples', 'theta', 'band', 'row')), parts along dimension 0
The draws below stay inside these ranges and needn't reach their ends.
There are 2 independent parts, one for each index of `samples`. The reference program is written for one: setup_inputs(seed, part) draws one part's arguments, and reference() takes and returns one part's arrays. A program takes and returns all parts, laid end to end along the dimension named above; an argument that names none is the same for every part. Nothing has to cross between parts.
All inputs are finite; a program needn't handle non-finite values.
Results may differ from the reference program's by a relative error of at most 0.0001.
Values sent between devices are 32-bit elements; how exact they have to be, the bound alone decides.
A program may use at most 64 MiB of HBM per device.

```python
import math
import jax
import jax.numpy as jnp
from jax import lax

FIELDS = 5
CT = 16
CA = 128
ITERS = 3
PATCH = 128
NT = 64
NR = 32
NPATCH = 32
MODES = 32
N_THETA = 4
N_ROW = 2


def set_ends(drawn, stream_key, low, top_value):
    place = [jax.random.randint(jax.random.fold_in(stream_key, axis), (), 0, length) for axis, length in enumerate(drawn.shape)]
    main_axis = drawn.shape.index(max(drawn.shape))
    beside = place[:main_axis] + [(place[main_axis] + 1) % drawn.shape[main_axis]] + place[main_axis + 1:]
    return drawn.at[tuple(place)].set(low).at[tuple(beside)].set(top_value)


def shard_levels(stream_key, dims, cuts, least, high):
    gain, own = 1.0, jax.random.fold_in(stream_key, 6)
    for axis_at, blocks in cuts:
        steps = jnp.exp(jax.random.uniform(jax.random.fold_in(own, axis_at), (blocks,), jnp.float32, least / len(cuts), high / len(cuts)))
        gain = gain * jnp.repeat(steps, dims[axis_at] // blocks).reshape([-1 if axis == axis_at else 1 for axis in range(len(dims))])
    return gain


def bell_draw(stream_key, extent, spread, bound, pieces=(), dtype=jnp.bfloat16):
    array = jax.random.normal(stream_key, extent, jnp.float32) * spread
    if len(pieces) > 0:
        array = shard_levels(stream_key, extent, pieces, -0.22, 0.18) * array
    return jnp.clip(array, min=-bound, max=bound).astype(dtype)


def setup_inputs(seed: int = 0, part: int = 0) -> dict:
    splits = jax.random.split(jax.random.key(seed), 11)
    own_keys = jax.random.split(jax.random.fold_in(splits[10], part), 11)
    adjoint = bell_draw(own_keys[0], (N_ROW, FIELDS, NT, NR, CA), 1.0, 6.0, ((0, 2), (2, 4), (3, 2)), jnp.float32)
    objective_grad = bell_draw(own_keys[1], (N_ROW, FIELDS, NT, NR, CA), 2.0, 12.0, ((0, 2), (2, 4), (3, 2)), jnp.float32)
    face_coef = jnp.clip(jnp.exp(math.log(2.0) - 1.3862944 * jax.random.uniform(own_keys[2], (N_ROW, 3, NT, NR, CA), jnp.float32) ** shard_levels(own_keys[2], (N_ROW, 3, NT, NR, CA), ((0, 2), (2, 4), (3, 2)), -0.2, 0.2)), 0.5, 2.0)
    source = jnp.clip(jnp.exp(math.log(4.0) - 2.0794415 * jax.random.uniform(own_keys[3], (N_ROW, NT, NR, CA), jnp.float32) ** shard_levels(own_keys[3], (N_ROW, NT, NR, CA), ((0, 2), (1, 4), (2, 2)), -0.2, 0.2)), 0.5, 4.0)
    flux_jac = bell_draw(splits[4], (N_ROW, 3, 2, FIELDS, FIELDS), FIELDS ** -0.5, 2.5, ((0, 2),), jnp.float32)
    mix_weight = jnp.clip(jnp.exp(math.log(1.0) - 1.3862944 * jax.random.uniform(own_keys[5], (N_ROW, NT, NR), jnp.float32) ** shard_levels(own_keys[5], (N_ROW, NT, NR), ((0, 2), (1, 4), (2, 2)), -0.2, 0.2)), 0.25, 1.0)
    mix_map = set_ends(jax.random.randint(own_keys[6], (N_ROW, NR), 0, NR), jax.random.fold_in(own_keys[6], 1), 0, NR - 1).astype(jnp.int32)
    mix_jac = bell_draw(splits[7], (N_ROW, FIELDS, FIELDS), FIELDS ** -0.5, 2.5, ((0, 2),), jnp.float32)
    surf_weight = bell_draw(own_keys[8], (N_ROW, FIELDS, N_THETA, NR, CA), 0.25, 1.5, ((0, 2), (2, 4), (3, 2)), jnp.float32)
    patch_mode = set_ends(jax.random.randint(own_keys[9], (N_ROW, N_THETA, NPATCH), 0, MODES), jax.random.fold_in(own_keys[9], 1), 0, MODES - 1).astype(jnp.int32)
    return dict(adjoint=adjoint, objective_grad=objective_grad, face_coef=face_coef, source=source, flux_jac=flux_jac, mix_weight=mix_weight, mix_map=mix_map, mix_jac=mix_jac, surf_weight=surf_weight, patch_mode=patch_mode)


OMEGA = 0.8


def lower_shift(values, axis):
    zero_layer = jnp.zeros_like(lax.slice_in_dim(values, 0, 1, axis=axis))
    return jnp.concatenate([zero_layer, lax.slice_in_dim(values, 0, values.shape[axis] - 1, axis=axis)], axis)


def upper_shift(values, axis):
    zero_layer = jnp.zeros_like(lax.slice_in_dim(values, 0, 1, axis=axis))
    return jnp.concatenate([lax.slice_in_dim(values, 1, values.shape[axis], axis=axis), zero_layer], axis)


def apply_block(matrix, values):
    return jnp.einsum("gf,gtra->ftra", matrix, values, precision=lax.Precision.HIGHEST)


def transposed_flux(center, uppers, lowers, coef_up, coef_low, jacobian):
    total = jnp.zeros_like(center)
    for direction in range(3):
        total = total + apply_block(jacobian[direction, 0], coef_up[direction][None] * (center - uppers[direction]))
        total = total + apply_block(jacobian[direction, 1], coef_low[direction][None] * (lowers[direction] - center))
    return total


def reference(adjoint, objective_grad, face_coef, source, flux_jac, mix_weight, mix_map, mix_jac, surf_weight, patch_mode):
    n_radial = adjoint.shape[3]
    n_axial = adjoint.shape[4]
    positions = jnp.arange(n_axial)
    face_index = (n_axial - 1, 0)
    lows = []
    diagonals = []
    onehots = []
    for blade in range(2):
        coef_up = (face_coef[blade, 0], face_coef[blade, 1], face_coef[blade, 2])
        coef_low = (jnp.roll(coef_up[0], 1, 0), lower_shift(coef_up[1], 1), lower_shift(coef_up[2], 2))
        lows.append(coef_low)
        diag_sum = source[blade]
        for direction in range(3):
            diag_sum = diag_sum + coef_up[direction] + coef_low[direction]
        diagonals.append(diag_sum)
        onehots.append((mix_map[blade][:, None] == jnp.arange(n_radial)[None, :]).astype(jnp.float32))
    fields = [adjoint[0], adjoint[1]]
    for step in range(ITERS):
        matched = []
        for blade in range(2):
            face_vals = fields[blade][:, :, :, face_index[blade]]
            face_sum = jnp.sum(face_vals * mix_weight[blade][None], axis=1)
            matched.append(jnp.dot(face_sum, onehots[blade], precision=lax.Precision.HIGHEST))
        updated = []
        for blade in range(2):
            center = fields[blade]
            uppers = (jnp.roll(center, -1, 1), upper_shift(center, 2), upper_shift(center, 3))
            lowers = (jnp.roll(center, 1, 1), lower_shift(center, 2), lower_shift(center, 3))
            coef_up = (face_coef[blade, 0], face_coef[blade, 1], face_coef[blade, 2])
            flux = transposed_flux(center, uppers, lowers, coef_up, lows[blade], flux_jac[blade])
            plane = jnp.einsum("gf,gr->fr", mix_jac[blade], matched[1 - blade], precision=lax.Precision.HIGHEST)
            axial_sel = (positions == face_index[blade]).astype(jnp.float32)
            resid = flux + plane[:, None, :, None] * axial_sel - objective_grad[blade]
            updated.append(center - OMEGA * resid / diagonals[blade])
        fields = updated
    adjoint_out = jnp.stack(fields)
    block_list = []
    for blade in range(2):
        surface = fields[blade][:, ::CT]
        weighted = jnp.sum(surf_weight[blade] * surface, axis=0)
        block_list.append(weighted.reshape(-1, PATCH))
    blocks = jnp.concatenate(block_list, 0)
    sensitivity = jax.ops.segment_sum(blocks, patch_mode.reshape(-1), MODES)
    return adjoint_out, sensitivity
```

```python
import functools

import jax
import jax.numpy as jnp
from jax import lax
from jax.experimental import pallas as pl
from jax.experimental.pallas import tpu as pltpu
from jax.sharding import PartitionSpec as P

ITERS = 3
OMEGA = 0.8
MESH = pl.DeviceIdType.MESH
F32 = jnp.float32
STEP = 2


def add_block(totals, jac, direction, side, values, sign=1.0):
    fields = len(values)
    for f in range(fields):
        for g in range(fields):
            term = jac[0, direction, side, g, f] * values[g]
            totals[f] = totals[f] + term if sign > 0 else totals[f] - term
    return totals


def kernel(
    sizes,
    adjoint,
    grad_hbm,
    coef_hbm,
    source_hbm,
    jac,
    weights,
    row_map,
    mix_jac,
    surf,
    modes,
    out,
    sens_out,
    field,
    coef,
    grad,
    scale,
    acc,
    theta_in,
    band_in,
    band_out,
    coef_theta,
    coef_band,
    coef_top,
    face_weight,
    one_hot,
    corr,
    plane,
    mix_out,
    mix_in,
    sens_part,
    sens_in,
    load_sem,
    send_sem,
    recv_sem,
    coef_send,
    coef_recv,
    mix_send,
    mix_recv,
    sens_send,
    sens_recv,
):
    n_theta, n_band, nf, nt, nr, na, own_modes = sizes
    group = n_theta * n_band * 2
    theta = lax.axis_index("theta")
    band = lax.axis_index("band")
    row = lax.axis_index("row")
    me = (theta * n_band + band) * 2 + row
    next_theta = lax.rem(theta + 1, n_theta)
    prev_theta = lax.rem(theta + n_theta - 1, n_theta)
    has_above = band < n_band - 1
    has_below = band > 0
    face = jnp.where(row == 0, na - 1, 0)

    def device(index):
        return {
            "theta": index // (2 * n_band),
            "band": lax.rem(index // 2, n_band),
            "row": lax.rem(index, 2),
        }

    def remote(src, dst, send, recv, **where):
        return pltpu.make_async_remote_copy(
            src_ref=src, dst_ref=dst, send_sem=send, recv_sem=recv,
            device_id=where, device_id_type=MESH,
        )

    loads = [
        pltpu.make_async_copy(adjoint.at[0], field.at[0, :, pl.ds(1, nt)], load_sem.at[0]),
        pltpu.make_async_copy(coef_hbm.at[0], coef.at[:, pl.ds(1, nt)], load_sem.at[1]),
        pltpu.make_async_copy(grad_hbm.at[0], grad, load_sem.at[2]),
        pltpu.make_async_copy(source_hbm.at[0], scale, load_sem.at[3]),
    ]
    for load in loads:
        load.start()

    barrier = pltpu.get_barrier_semaphore()

    def greet(i, carry):
        pl.semaphore_signal(
            barrier, inc=1, device_id=device(lax.rem(me + i, group)), device_id_type=MESH
        )
        return carry

    lax.fori_loop(1, group, greet, 0)

    layer = jnp.zeros((nr, na), F32)
    for k in range(ITERS):
        for f in range(nf):
            field[k, f, 0] = layer
            field[k, f, nt + 1] = layer
    coef[0, 0] = layer

    @pl.when(jnp.logical_not(has_above))
    def _():
        for k in range(ITERS):
            band_in[k, 1] = jnp.zeros((nf, nt, na), F32)

    @pl.when(jnp.logical_not(has_below))
    def _():
        for k in range(ITERS):
            band_in[k, 0] = jnp.zeros((nf, nt, na), F32)
        coef_band[...] = jnp.zeros((nt, na), F32)

    lanes = lax.broadcasted_iota(jnp.int32, (nr, na), 1)
    rows = lax.broadcasted_iota(jnp.int32, (nr, na), 0)
    at_face = lanes == face
    row_lanes = lax.broadcasted_iota(jnp.int32, (1, na), 1)
    eye = lax.broadcasted_iota(jnp.int32, (nr, nr), 0) == lax.broadcasted_iota(
        jnp.int32, (nr, nr), 1
    )
    for q in range(nr):
        one_hot[pl.ds(q, 1), :] = jnp.where(row_lanes == row_map[0, q], 1.0, 0.0)
    for t in range(nt):
        line = jnp.broadcast_to(weights[0, pl.ds(t, 1), :], (nr, nr))
        column = jnp.sum(jnp.where(eye, line, 0.0), axis=1, keepdims=True)
        face_weight[t] = jnp.where(at_face, column, 0.0)

    loads[0].wait()
    loads[1].wait()

    def pack(t, sums):
        result = []
        for f in range(nf):
            value = field[0, f, t + 1]
            band_out[0, 0, f, pl.ds(t, 1), :] = value[:1]
            band_out[0, 1, f, pl.ds(t, 1), :] = value[nr - 1 :]
            result.append(sums[f] + face_weight[t] * value)
        coef_top[pl.ds(t, 1), :] = coef[1, t + 1, pl.ds(nr - 1, 1), :]
        return tuple(result)

    def halo_copies(k):
        theta_copies = [
            remote(field.at[k, :, nt], theta_in.at[k, 0], send_sem.at[k, 0],
                   recv_sem.at[k, 0], theta=next_theta),
            remote(field.at[k, :, 1], theta_in.at[k, 1], send_sem.at[k, 1],
                   recv_sem.at[k, 1], theta=prev_theta),
        ]
        up = remote(band_out.at[k, 1], band_in.at[k, 0], send_sem.at[k, 2],
                    recv_sem.at[k, 2], band=band + 1)
        down = remote(band_out.at[k, 0], band_in.at[k, 1], send_sem.at[k, 3],
                      recv_sem.at[k, 3], band=band - 1)
        return theta_copies, up, down

    def mix_copies(k, start):
        slot = theta * n_band + band

        def one(i, carry):
            to = lax.rem(slot + i, n_theta * n_band)
            remote(mix_out.at[k], mix_in.at[k, slot], mix_send.at[k], mix_recv.at[k],
                   theta=to // n_band, band=lax.rem(to, n_band), row=1 - row).start()
            return carry

        lax.fori_loop(0, n_theta * n_band, one, 0)

    def send_mix(k, sums):
        hot = one_hot[...]
        for f in range(nf):
            column = jnp.sum(sums[f], axis=1, keepdims=True)
            mix_out[k, pl.ds(f, 1), :] = jnp.sum(hot * column, axis=0, keepdims=True)
        mix_copies(k, True)

    def start_halos(k):
        theta_copies, up, down = halo_copies(k)
        pl.when(has_above)(up.start)
        pl.when(has_below)(down.start)
        for copy in theta_copies:
            copy.start()

    zero_sums = tuple(jnp.zeros((nr, na), F32) for _ in range(nf))
    for k in range(ITERS):
        mix_out[k] = jnp.zeros((8, na), F32)
    sums = lax.fori_loop(0, nt, pack, zero_sums)

    pl.semaphore_wait(barrier, group - 1)
    coef_up = remote(coef_top, coef_band, coef_send.at[1], coef_recv.at[1], band=band + 1)
    coef_next = remote(coef.at[0, nt], coef_theta, coef_send.at[0], coef_recv.at[0],
                       theta=next_theta)
    send_mix(0, sums)
    start_halos(0)
    coef_next.start()
    pl.when(has_above)(coef_up.start)
    loads[2].wait()
    loads[3].wait()

    chunk_lanes = lax.broadcasted_iota(jnp.int32, (STEP, nr, na), 2)
    chunk_rows = lax.broadcasted_iota(jnp.int32, (STEP, nr, na), 1)

    def lane_up(v):
        return jnp.where(chunk_lanes == na - 1, 0.0, pltpu.roll(v, na - 1, 2))

    def lane_down(v):
        return jnp.where(chunk_lanes == 0, 0.0, pltpu.roll(v, 1, 2))

    def row_up(v):
        return jnp.where(chunk_rows == nr - 1, 0.0, pltpu.roll(v, nr - 1, 1))

    def row_down(v):
        return jnp.where(chunk_rows == 0, 0.0, pltpu.roll(v, 1, 1))

    for k in range(ITERS):

        def bulk(i, carry):
            t = i * STEP
            own = pl.ds(t + 1, STEP)
            total = [-grad[f, pl.ds(t, STEP)] for f in range(nf)]
            c_axial = coef[2, own]
            w = []
            for f in range(nf):
                v = field[k, f, own]
                w.append(c_axial * (v - lane_up(v)))
            total = add_block(total, jac, 2, 0, w)
            total = add_block(total, jac, 2, 1, [lane_down(x) for x in w])
            c_radial = coef[1, own]
            w = []
            for f in range(nf):
                v = field[k, f, own]
                w.append(c_radial * (v - row_up(v)))
            total = add_block(total, jac, 1, 0, w)
            total = add_block(total, jac, 1, 1, [row_down(x) for x in w])
            c_theta = coef[0, pl.ds(t, STEP + 1)]
            w = []
            for f in range(nf):
                v = field[k, f, pl.ds(t, STEP + 2)]
                w.append(c_theta * (v[: STEP + 1] - v[1:]))
            total = add_block(total, jac, 0, 0, [x[1:] for x in w])
            total = add_block(total, jac, 0, 1, [x[:STEP] for x in w])
            for f in range(nf):
                acc[f, pl.ds(t, STEP)] = total[f]
            if k == 0:
                low = row_down(c_radial) + lane_down(c_axial)
                scale[pl.ds(t, STEP)] = (
                    scale[pl.ds(t, STEP)] + c_theta[1:] + c_theta[:STEP] + c_radial + c_axial + low
                )
            return carry

        lax.fori_loop(0, nt // STEP, bulk, 0)

        theta_copies, up, down = halo_copies(k)
        for copy in theta_copies:
            copy.wait()
        if k == 0:
            coef_next.wait()

            @pl.when(has_above)
            def _():
                coef_up.wait_send()

            @pl.when(has_below)
            def _():
                coef_up.wait_recv()

            scale[0] += coef_theta[...]
        before = [coef_theta[...] * (theta_in[k, 0, f] - field[k, f, 1]) for f in range(nf)]
        total = add_block([acc[f, 0] for f in range(nf)], jac, 0, 1, before)
        for f in range(nf):
            acc[f, 0] = total[f]
        after = [coef[0, nt] * theta_in[k, 1, f] for f in range(nf)]
        total = add_block([acc[f, nt - 1] for f in range(nf)], jac, 0, 0, after, -1.0)
        for f in range(nf):
            acc[f, nt - 1] = total[f]

        @pl.when(has_above)
        def _():
            up.wait_send()
            down.wait_recv()

        @pl.when(has_below)
        def _():
            down.wait_send()
            up.wait_recv()

        flat = jnp.zeros((nt, na), F32)
        below = [coef_band[...] * (band_in[k, 0, f] - band_out[k, 0, f]) for f in range(nf)]
        total = add_block([flat] * nf, jac, 1, 1, below)
        above = [coef_top[...] * band_in[k, 1, f] for f in range(nf)]
        other = add_block([flat] * nf, jac, 1, 0, above, -1.0)
        for f in range(nf):
            corr[0, f] = total[f]
            corr[1, f] = other[f]

        pltpu.make_async_copy(mix_in.at[k], mix_in.at[k], mix_recv.at[k]).wait()
        pltpu.make_async_copy(mix_in.at[k], mix_in.at[k], mix_send.at[k]).wait()
        matched = lax.fori_loop(
            1, n_theta * n_band, lambda i, m: m + mix_in[k, i], mix_in[k, 0]
        )
        here = lanes == rows + band * nr
        for f in range(nf):
            line = mix_jac[0, 0, f] * matched[:1]
            for g in range(1, nf):
                line = line + mix_jac[0, g, f] * matched[g : g + 1]
            column = jnp.sum(jnp.where(here, line, 0.0), axis=1, keepdims=True)
            plane[f] = jnp.where(at_face, column, 0.0)

        def finish(t, sums):
            if k == 0:
                bottom = jnp.where(rows == 0, coef_band[pl.ds(t, 1), :], 0.0)
                gain = OMEGA / (scale[t] + bottom)
                scale[t] = gain
            else:
                gain = scale[t]
            result = []
            for f in range(nf):
                resid = acc[f, t] + plane[f]
                resid = resid + jnp.where(rows == 0, corr[0, f, pl.ds(t, 1), :], 0.0)
                resid = resid + jnp.where(rows == nr - 1, corr[1, f, pl.ds(t, 1), :], 0.0)
                value = field[k, f, t + 1] - gain * resid
                if k < ITERS - 1:
                    field[k + 1, f, t + 1] = value
                    band_out[k + 1, 0, f, pl.ds(t, 1), :] = value[:1]
                    band_out[k + 1, 1, f, pl.ds(t, 1), :] = value[nr - 1 :]
                    result.append(sums[f] + face_weight[t] * value)
                else:
                    out[0, f, t] = value
            return tuple(result) if k < ITERS - 1 else sums

        if k < ITERS - 1:
            sums = lax.fori_loop(0, nt, finish, zero_sums)
            send_mix(k + 1, sums)
            start_halos(k + 1)
        else:
            finish(0, 0)
            weighted = surf[0, 0, 0] * out[0, 0, 0]
            for f in range(1, nf):
                weighted = weighted + surf[0, f, 0] * out[0, f, 0]
            tile_rows = lax.broadcasted_iota(jnp.int32, (8, na), 0)

            def part(d, carry):
                mode = jnp.where(tile_rows < own_modes, tile_rows + d * own_modes, -1)
                total = jnp.zeros((8, na), F32)
                for r in range(nr):
                    total = total + jnp.where(mode == modes[0, 0, r], weighted[r : r + 1], 0.0)
                sens_part[d] = total
                return carry

            lax.fori_loop(0, group, part, 0)

            def send(i, carry):
                to = lax.rem(me + i, group)
                remote(sens_part.at[to], sens_in.at[i - 1], sens_send.at[0], sens_recv.at[0],
                       **device(to)).start()
                return carry

            lax.fori_loop(1, group, send, 0)
            lax.fori_loop(1, nt, finish, 0)
            pltpu.make_async_copy(sens_in, sens_in, sens_recv.at[0]).wait()
            pltpu.make_async_copy(sens_in, sens_in, sens_send.at[0]).wait()
            total = lax.fori_loop(0, group - 1, lambda i, s: s + sens_in[i], sens_part[me])
            sens_out[...] = total[:own_modes]


def local(sizes, *args):
    adjoint = args[0]
    n_theta, n_band, own_modes = sizes
    _, nf, nt, nr, na = adjoint.shape
    group = n_theta * n_band * 2
    dma = pltpu.SemaphoreType.DMA
    any_space = pl.BlockSpec(memory_space=pl.ANY)
    vmem = pl.BlockSpec(memory_space=pltpu.VMEM)
    smem = pl.BlockSpec(memory_space=pltpu.SMEM)
    return pl.pallas_call(
        functools.partial(kernel, (n_theta, n_band, nf, nt, nr, na, own_modes)),
        out_shape=(
            jax.ShapeDtypeStruct(adjoint.shape, F32),
            jax.ShapeDtypeStruct((own_modes, na), F32),
        ),
        in_specs=[any_space] * 4 + [smem, vmem, smem, smem, vmem, smem],
        out_specs=(vmem, vmem),
        scratch_shapes=[
            pltpu.VMEM((ITERS, nf, nt + 2, nr, na), F32),
            pltpu.VMEM((3, nt + 1, nr, na), F32),
            pltpu.VMEM((nf, nt, nr, na), F32),
            pltpu.VMEM((nt, nr, na), F32),
            pltpu.VMEM((nf, nt, nr, na), F32),
            pltpu.VMEM((ITERS, 2, nf, nr, na), F32),
            pltpu.VMEM((ITERS, 2, nf, nt, na), F32),
            pltpu.VMEM((ITERS, 2, nf, nt, na), F32),
            pltpu.VMEM((nr, na), F32),
            pltpu.VMEM((nt, na), F32),
            pltpu.VMEM((nt, na), F32),
            pltpu.VMEM((nt, nr, na), F32),
            pltpu.VMEM((nr, na), F32),
            pltpu.VMEM((2, nf, nt, na), F32),
            pltpu.VMEM((nf, nr, na), F32),
            pltpu.VMEM((ITERS, 8, na), F32),
            pltpu.VMEM((ITERS, n_theta * n_band, 8, na), F32),
            pltpu.VMEM((group, 8, na), F32),
            pltpu.VMEM((group - 1, 8, na), F32),
            dma((4,)),
            dma((ITERS, 4)),
            dma((ITERS, 4)),
            dma((2,)),
            dma((2,)),
            dma((ITERS,)),
            dma((ITERS,)),
            dma((1,)),
            dma((1,)),
        ],
        compiler_params=pltpu.CompilerParams(
            collective_id=0, has_side_effects=True, vmem_limit_bytes=40 * 1024 * 1024
        ),
    )(*args)


def solution(mesh):
    cells = P(("samples", "row"), None, "theta", "band", None)
    placed = (
        cells,
        cells,
        cells,
        P(("samples", "row"), "theta", "band", None),
        P("row", None, None, None, None),
        P(("samples", "row"), "theta", "band"),
        P(("samples", "row"), "band"),
        P("row", None, None),
        cells,
        P(("samples", "row"), "theta", "band"),
    )
    return jax.shard_map(
        functools.partial(local, (mesh.shape["theta"], mesh.shape["band"], 2)),
        mesh=mesh,
        in_specs=placed,
        out_specs=(cells, P(("samples", "theta", "band", "row"), None)),
        check_vma=False,
    )
```

```python
import functools

import jax
import jax.numpy as jnp
from jax import lax
from jax.experimental import pallas as pl
from jax.experimental.pallas import tpu as pltpu
from jax.sharding import PartitionSpec as P

ITERS = 3
OMEGA = 0.8
MESH = pl.DeviceIdType.MESH
F32 = jnp.float32
STEP = 2


def add_block(totals, jac, direction, side, values, sign=1.0):
    fields = len(values)
    for f in range(fields):
        for g in range(fields):
            term = jac[0, direction, g, side, f] * values[g]
            totals[f] = totals[f] + term if sign > 0 else totals[f] - term
    return totals


def kernel(
    sizes,
    adjoint,
    grad_hbm,
    coef_hbm,
    source_hbm,
    jac,
    weights_hbm,
    row_map,
    mix_jac,
    surf_hbm,
    modes,
    out,
    sens_out,
    field,
    coef,
    grad,
    scale,
    acc,
    theta_in,
    band_in,
    band_out,
    coef_theta,
    coef_band,
    coef_top,
    face_weight,
    one_hot,
    corr,
    plane,
    mix_out,
    mix_in,
    sens_part,
    sens_in,
    weights,
    surf,
    load_sem,
    send_sem,
    recv_sem,
    coef_send,
    coef_recv,
    mix_send,
    mix_recv,
    sens_send,
    sens_recv,
):
    n_theta, n_band, nf, nt, nr, na, own_modes = sizes
    group = n_theta * n_band * 2
    theta = lax.axis_index("theta")
    band = lax.axis_index("band")
    row = lax.axis_index("row")
    me = (theta * n_band + band) * 2 + row
    next_theta = lax.rem(theta + 1, n_theta)
    prev_theta = lax.rem(theta + n_theta - 1, n_theta)
    has_above = band < n_band - 1
    has_below = band > 0
    face = jnp.where(row == 0, na - 1, 0)

    def device(index):
        return {
            "theta": index // (2 * n_band),
            "band": lax.rem(index // 2, n_band),
            "row": lax.rem(index, 2),
        }

    def remote(src, dst, send, recv, **where):
        return pltpu.make_async_remote_copy(
            src_ref=src, dst_ref=dst, send_sem=send, recv_sem=recv,
            device_id=where, device_id_type=MESH,
        )

    loads = [
        pltpu.make_async_copy(adjoint.at[0], field.at[0, :, pl.ds(1, nt)], load_sem.at[0]),
        pltpu.make_async_copy(coef_hbm.at[0], coef.at[:, pl.ds(1, nt)], load_sem.at[1]),
        pltpu.make_async_copy(grad_hbm.at[0], grad, load_sem.at[2]),
        pltpu.make_async_copy(source_hbm.at[0], scale, load_sem.at[3]),
        pltpu.make_async_copy(weights_hbm, weights, load_sem.at[4]),
        pltpu.make_async_copy(surf_hbm, surf, load_sem.at[5]),
    ]
    for load in loads:
        load.start()

    barrier = pltpu.get_barrier_semaphore()

    def greet(i, carry):
        pl.semaphore_signal(
            barrier, inc=1, device_id=device(lax.rem(me + i, group)), device_id_type=MESH
        )
        return carry

    lax.fori_loop(1, group, greet, 0)

    layer = jnp.zeros((nr, na), F32)
    for k in range(ITERS):
        for f in range(nf):
            field[k, f, 0] = layer
            field[k, f, nt + 1] = layer
    coef[0, 0] = layer

    @pl.when(jnp.logical_not(has_above))
    def _():
        for k in range(ITERS):
            band_in[k, 1] = jnp.zeros((nf, nt, na), F32)

    @pl.when(jnp.logical_not(has_below))
    def _():
        for k in range(ITERS):
            band_in[k, 0] = jnp.zeros((nf, nt, na), F32)
        coef_band[...] = jnp.zeros((nt, na), F32)

    lanes = lax.broadcasted_iota(jnp.int32, (nr, na), 1)
    rows = lax.broadcasted_iota(jnp.int32, (nr, na), 0)
    at_face = lanes == face
    row_lanes = lax.broadcasted_iota(jnp.int32, (1, na), 1)
    eye = lax.broadcasted_iota(jnp.int32, (nr, nr), 0) == lax.broadcasted_iota(
        jnp.int32, (nr, nr), 1
    )
    for q in range(nr):
        one_hot[pl.ds(q, 1), :] = jnp.where(row_lanes == row_map[0, q], 1.0, 0.0)
    loads[4].wait()
    for t in range(nt):
        line = jnp.broadcast_to(weights[0, pl.ds(t, 1), :], (nr, nr))
        column = jnp.sum(jnp.where(eye, line, 0.0), axis=1, keepdims=True)
        face_weight[t] = jnp.where(at_face, column, 0.0)

    loads[0].wait()
    loads[1].wait()

    def pack(t, sums):
        result = []
        for f in range(nf):
            value = field[0, f, t + 1]
            band_out[0, 0, f, pl.ds(t, 1), :] = value[:1]
            band_out[0, 1, f, pl.ds(t, 1), :] = value[nr - 1 :]
            result.append(sums[f] + face_weight[t] * value)
        coef_top[pl.ds(t, 1), :] = coef[1, t + 1, pl.ds(nr - 1, 1), :]
        return tuple(result)

    def halo_copies(k):
        theta_copies = [
            remote(field.at[k, :, nt], theta_in.at[k, 0], send_sem.at[k, 0],
                   recv_sem.at[k, 0], theta=next_theta),
            remote(field.at[k, :, 1], theta_in.at[k, 1], send_sem.at[k, 1],
                   recv_sem.at[k, 1], theta=prev_theta),
        ]
        up = remote(band_out.at[k, 1], band_in.at[k, 0], send_sem.at[k, 2],
                    recv_sem.at[k, 2], band=band + 1)
        down = remote(band_out.at[k, 0], band_in.at[k, 1], send_sem.at[k, 3],
                      recv_sem.at[k, 3], band=band - 1)
        return theta_copies, up, down

    def mix_copies(k, start):
        slot = theta * n_band + band

        def one(i, carry):
            to = lax.rem(slot + i, n_theta * n_band)
            remote(mix_out.at[k], mix_in.at[k, slot], mix_send.at[k], mix_recv.at[k],
                   theta=to // n_band, band=lax.rem(to, n_band), row=1 - row).start()
            return carry

        lax.fori_loop(0, n_theta * n_band, one, 0)

    def send_mix(k, sums):
        hot = one_hot[...]
        for f in range(nf):
            column = jnp.sum(sums[f], axis=1, keepdims=True)
            mix_out[k, pl.ds(f, 1), :] = jnp.sum(hot * column, axis=0, keepdims=True)
        mix_copies(k, True)

    def start_theta(k):
        for copy in halo_copies(k)[0]:
            copy.start()

    def start_band(k):
        _, up, down = halo_copies(k)
        pl.when(has_above)(up.start)
        pl.when(has_below)(down.start)

    zero_sums = tuple(jnp.zeros((nr, na), F32) for _ in range(nf))
    for k in range(ITERS):
        mix_out[k] = jnp.zeros((8, na), F32)
    pl.semaphore_wait(barrier, group - 1)
    coef_up = remote(coef_top, coef_band, coef_send.at[1], coef_recv.at[1], band=band + 1)
    coef_next = remote(coef.at[0, nt], coef_theta, coef_send.at[0], coef_recv.at[0],
                       theta=next_theta)
    start_theta(0)
    coef_next.start()
    sums = lax.fori_loop(0, nt, pack, zero_sums)
    send_mix(0, sums)
    start_band(0)
    pl.when(has_above)(coef_up.start)
    loads[2].wait()
    loads[3].wait()
    loads[5].wait()

    chunk_lanes = lax.broadcasted_iota(jnp.int32, (STEP, nr, na), 2)
    chunk_rows = lax.broadcasted_iota(jnp.int32, (STEP, nr, na), 1)

    def lane_up(v):
        return jnp.where(chunk_lanes == na - 1, 0.0, pltpu.roll(v, na - 1, 2))

    def lane_down(v):
        return jnp.where(chunk_lanes == 0, 0.0, pltpu.roll(v, 1, 2))

    def row_up(v):
        return jnp.where(chunk_rows == nr - 1, 0.0, pltpu.roll(v, nr - 1, 1))

    def row_down(v):
        return jnp.where(chunk_rows == 0, 0.0, pltpu.roll(v, 1, 1))

    for k in range(ITERS):

        def bulk(i, carry):
            t = i * STEP
            own = pl.ds(t + 1, STEP)
            total = [-grad[f, pl.ds(t, STEP)] for f in range(nf)]
            c_axial = coef[2, own]
            w = []
            for f in range(nf):
                v = field[k, f, own]
                w.append(c_axial * (v - lane_up(v)))
            total = add_block(total, jac, 2, 0, w)
            total = add_block(total, jac, 2, 1, [lane_down(x) for x in w])
            c_radial = coef[1, own]
            w = []
            for f in range(nf):
                v = field[k, f, own]
                w.append(c_radial * (v - row_up(v)))
            total = add_block(total, jac, 1, 0, w)
            total = add_block(total, jac, 1, 1, [row_down(x) for x in w])
            c_theta = coef[0, pl.ds(t, STEP + 1)]
            w = []
            for f in range(nf):
                v = field[k, f, pl.ds(t, STEP + 2)]
                w.append(c_theta * (v[: STEP + 1] - v[1:]))
            total = add_block(total, jac, 0, 0, [x[1:] for x in w])
            total = add_block(total, jac, 0, 1, [x[:STEP] for x in w])
            for f in range(nf):
                acc[f, pl.ds(t, STEP)] = total[f]
            if k == 0:
                low = row_down(c_radial) + lane_down(c_axial)
                scale[pl.ds(t, STEP)] = (
                    scale[pl.ds(t, STEP)] + c_theta[1:] + c_theta[:STEP] + c_radial + c_axial + low
                )
            return carry

        lax.fori_loop(0, nt // STEP, bulk, 0)

        theta_copies, up, down = halo_copies(k)
        pltpu.make_async_copy(mix_in.at[k], mix_in.at[k], mix_recv.at[k]).wait()
        pltpu.make_async_copy(mix_in.at[k], mix_in.at[k], mix_send.at[k]).wait()
        matched = lax.fori_loop(
            1, n_theta * n_band, lambda i, m: m + mix_in[k, i], mix_in[k, 0]
        )
        here = lanes == rows + band * nr
        for f in range(nf):
            line = mix_jac[0, 0, f] * matched[:1]
            for g in range(1, nf):
                line = line + mix_jac[g, 0, f] * matched[g : g + 1]
            column = jnp.sum(jnp.where(here, line, 0.0), axis=1, keepdims=True)
            plane[f] = jnp.where(at_face, column, 0.0)

        @pl.when(has_above)
        def _():
            up.wait_send()
            down.wait_recv()

        @pl.when(has_below)
        def _():
            down.wait_send()
            up.wait_recv()

        if k == 0:

            @pl.when(has_above)
            def _():
                coef_up.wait_send()

            @pl.when(has_below)
            def _():
                coef_up.wait_recv()

        flat = jnp.zeros((nt, na), F32)
        below = [coef_band[...] * (band_in[k, 0, f] - band_out[k, 0, f]) for f in range(nf)]
        total = add_block([flat] * nf, jac, 1, 1, below)
        above = [coef_top[...] * band_in[k, 1, f] for f in range(nf)]
        other = add_block([flat] * nf, jac, 1, 0, above, -1.0)
        for f in range(nf):
            corr[0, f] = total[f]
            corr[1, f] = other[f]

        for copy in theta_copies:
            copy.wait()
        if k == 0:
            coef_next.wait()

            scale[0] += coef_theta[...]
        before = [coef_theta[...] * (theta_in[k, 0, f] - field[k, f, 1]) for f in range(nf)]
        total = add_block([acc[f, 0] for f in range(nf)], jac, 0, 1, before)
        for f in range(nf):
            acc[f, 0] = total[f]
        after = [coef[0, nt] * theta_in[k, 1, f] for f in range(nf)]
        total = add_block([acc[f, nt - 1] for f in range(nf)], jac, 0, 0, after, -1.0)
        for f in range(nf):
            acc[f, nt - 1] = total[f]

        def finish(t, sums):
            if k == 0:
                bottom = jnp.where(rows == 0, coef_band[pl.ds(t, 1), :], 0.0)
                gain = OMEGA / (scale[t] + bottom)
                scale[t] = gain
            else:
                gain = scale[t]
            result = []
            for f in range(nf):
                resid = acc[f, t] + plane[f]
                resid = resid + jnp.where(rows == 0, corr[0, f, pl.ds(t, 1), :], 0.0)
                resid = resid + jnp.where(rows == nr - 1, corr[1, f, pl.ds(t, 1), :], 0.0)
                value = field[k, f, t + 1] - gain * resid
                if k < ITERS - 1:
                    field[k + 1, f, t + 1] = value
                    band_out[k + 1, 0, f, pl.ds(t, 1), :] = value[:1]
                    band_out[k + 1, 1, f, pl.ds(t, 1), :] = value[nr - 1 :]
                    result.append(sums[f] + face_weight[t] * value)
                else:
                    out[0, f, t] = value
            return tuple(result) if k < ITERS - 1 else sums

        if k < ITERS - 1:
            sums = lax.fori_loop(0, nt, finish, zero_sums)
            send_mix(k + 1, sums)
            start_band(k + 1)
            start_theta(k + 1)
        else:
            finish(0, 0)
            weighted = surf[0, 0, 0] * out[0, 0, 0]
            for f in range(1, nf):
                weighted = weighted + surf[0, f, 0] * out[0, f, 0]
            tile_rows = lax.broadcasted_iota(jnp.int32, (8, na), 0)

            owners = 8 // own_modes

            def part(d, carry):
                mode = tile_rows + d * 8
                total = jnp.zeros((8, na), F32)
                for r in range(nr):
                    total = total + jnp.where(mode == modes[0, 0, r], weighted[r : r + 1], 0.0)
                for j in range(owners):
                    sens_part[d * owners + j] = total[j * own_modes : (j + 1) * own_modes]
                return carry

            lax.fori_loop(0, group // owners, part, 0)

            def send(i, carry):
                to = lax.rem(me + i, group)
                remote(sens_part.at[to], sens_in.at[i - 1], sens_send.at[0], sens_recv.at[0],
                       **device(to)).start()
                return carry

            lax.fori_loop(1, group, send, 0)
            lax.fori_loop(1, nt, finish, 0)
            pltpu.make_async_copy(sens_in, sens_in, sens_recv.at[0]).wait()
            pltpu.make_async_copy(sens_in, sens_in, sens_send.at[0]).wait()
            total = lax.fori_loop(0, group - 1, lambda i, s: s + sens_in[i], sens_part[me])
            sens_out[...] = total


def local(sizes, *args):
    adjoint = args[0]
    n_theta, n_band, own_modes = sizes
    _, nf, nt, nr, na = adjoint.shape
    group = n_theta * n_band * 2
    dma = pltpu.SemaphoreType.DMA
    hbm = pl.BlockSpec(memory_space=pltpu.HBM)
    vmem = pl.BlockSpec(memory_space=pltpu.VMEM)
    smem = pl.BlockSpec(memory_space=pltpu.SMEM)
    return pl.pallas_call(
        functools.partial(kernel, (n_theta, n_band, nf, nt, nr, na, own_modes)),
        out_shape=(
            pltpu.VMEM(adjoint.shape, F32),
            pltpu.VMEM((own_modes, na), F32),
        ),
        in_specs=[hbm] * 4 + [smem, hbm, smem, smem, hbm, smem],
        out_specs=(vmem, vmem),
        scratch_shapes=[
            pltpu.VMEM((ITERS, nf, nt + 2, nr, na), F32),
            pltpu.VMEM((3, nt + 1, nr, na), F32),
            pltpu.VMEM((nf, nt, nr, na), F32),
            pltpu.VMEM((nt, nr, na), F32),
            pltpu.VMEM((nf, nt, nr, na), F32),
            pltpu.VMEM((ITERS, 2, nf, nr, na), F32),
            pltpu.VMEM((ITERS, 2, nf, nt, na), F32),
            pltpu.VMEM((ITERS, 2, nf, nt, na), F32),
            pltpu.VMEM((nr, na), F32),
            pltpu.VMEM((nt, na), F32),
            pltpu.VMEM((nt, na), F32),
            pltpu.VMEM((nt, nr, na), F32),
            pltpu.VMEM((nr, na), F32),
            pltpu.VMEM((2, nf, nt, na), F32),
            pltpu.VMEM((nf, nr, na), F32),
            pltpu.VMEM((ITERS, 8, na), F32),
            pltpu.VMEM((ITERS, n_theta * n_band, 8, na), F32),
            pltpu.VMEM((group, own_modes, na), F32),
            pltpu.VMEM((group - 1, own_modes, na), F32),
            pltpu.VMEM((1, nt, nr), F32),
            pltpu.VMEM((1, nf, 1, nr, na), F32),
            dma((6,)),
            dma((ITERS, 4)),
            dma((ITERS, 4)),
            dma((2,)),
            dma((2,)),
            dma((ITERS,)),
            dma((ITERS,)),
            dma((1,)),
            dma((1,)),
        ],
        compiler_params=pltpu.CompilerParams(
            collective_id=0, has_side_effects=True, vmem_limit_bytes=63 * 1024 * 1024
        ),
    )(*args[:4], jnp.swapaxes(args[4], 2, 3), *args[5:7], jnp.swapaxes(args[7], 0, 1), *args[8:])


def solution(mesh):
    cells = P(("samples", "row"), None, "theta", "band", None)
    placed = (
        cells,
        cells,
        cells,
        P(("samples", "row"), "theta", "band", None),
        P("row", None, None, None, None),
        P(("samples", "row"), "theta", "band"),
        P(("samples", "row"), "band"),
        P("row", None, None),
        cells,
        P(("samples", "row"), "theta", "band"),
    )
    return jax.shard_map(
        functools.partial(local, (mesh.shape["theta"], mesh.shape["band"], 2)),
        mesh=mesh,
        in_specs=placed,
        out_specs=(cells, P(("samples", "theta", "band", "row"), None)),
        check_vma=False,
    )
```

```python
import functools

import jax
import jax.numpy as jnp
from jax import lax
from jax.experimental import pallas as pl
from jax.experimental.pallas import tpu as pltpu
from jax.sharding import PartitionSpec as P

ITERS = 3
OMEGA = 0.8
MESH = pl.DeviceIdType.MESH
F32 = jnp.float32
STEP = 2


def add_block(totals, jac, direction, side, values, sign=1.0):
    fields = len(values)
    for f in range(fields):
        for g in range(fields):
            term = jac[0, direction, g, side, f] * values[g]
            totals[f] = totals[f] + term if sign > 0 else totals[f] - term
    return totals


def kernel(
    sizes,
    adjoint,
    grad_hbm,
    coef_hbm,
    source_hbm,
    jac,
    weights_hbm,
    row_map,
    mix_jac,
    surf_hbm,
    modes,
    out,
    sens_out,
    field,
    coef,
    grad,
    scale,
    acc,
    theta_in,
    band_in,
    band_out,
    coef_theta,
    coef_band,
    coef_top,
    face_weight,
    one_hot,
    corr,
    plane,
    mix_out,
    mix_in,
    sens_part,
    sens_in,
    weights,
    surf,
    load_sem,
    send_sem,
    recv_sem,
    coef_send,
    coef_recv,
    mix_send,
    mix_recv,
    sens_send,
    sens_recv,
):
    n_theta, n_band, nf, nt, nr, na, own_modes = sizes
    group = n_theta * n_band * 2
    theta = lax.axis_index("theta")
    band = lax.axis_index("band")
    row = lax.axis_index("row")
    me = (theta * n_band + band) * 2 + row
    next_theta = lax.rem(theta + 1, n_theta)
    prev_theta = lax.rem(theta + n_theta - 1, n_theta)
    has_above = band < n_band - 1
    has_below = band > 0
    face = jnp.where(row == 0, na - 1, 0)

    def device(index):
        return {
            "theta": index // (2 * n_band),
            "band": lax.rem(index // 2, n_band),
            "row": lax.rem(index, 2),
        }

    def remote(src, dst, send, recv, **where):
        return pltpu.make_async_remote_copy(
            src_ref=src, dst_ref=dst, send_sem=send, recv_sem=recv,
            device_id=where, device_id_type=MESH,
        )

    loads = [
        pltpu.make_async_copy(adjoint.at[0], field.at[0, :, pl.ds(1, nt)], load_sem.at[0]),
        pltpu.make_async_copy(coef_hbm.at[0], coef.at[:, pl.ds(1, nt)], load_sem.at[1]),
        pltpu.make_async_copy(grad_hbm.at[0], grad, load_sem.at[2]),
        pltpu.make_async_copy(source_hbm.at[0], scale, load_sem.at[3]),
        pltpu.make_async_copy(weights_hbm, weights, load_sem.at[4]),
        pltpu.make_async_copy(surf_hbm, surf, load_sem.at[5]),
    ]
    for load in loads:
        load.start()

    barrier = pltpu.get_barrier_semaphore()

    def greet(i, carry):
        pl.semaphore_signal(
            barrier, inc=1, device_id=device(lax.rem(me + i, group)), device_id_type=MESH
        )
        return carry

    lax.fori_loop(1, group, greet, 0)

    layer = jnp.zeros((nr, na), F32)
    for k in range(ITERS):
        for f in range(nf):
            field[k, f, 0] = layer
            field[k, f, nt + 1] = layer
    coef[0, 0] = layer

    @pl.when(jnp.logical_not(has_above))
    def _():
        for k in range(ITERS):
            band_in[k, 1] = jnp.zeros((nf, nt, na), F32)

    @pl.when(jnp.logical_not(has_below))
    def _():
        for k in range(ITERS):
            band_in[k, 0] = jnp.zeros((nf, nt, na), F32)
        coef_band[...] = jnp.zeros((nt, na), F32)

    lanes = lax.broadcasted_iota(jnp.int32, (nr, na), 1)
    rows = lax.broadcasted_iota(jnp.int32, (nr, na), 0)
    at_face = lanes == face
    row_lanes = lax.broadcasted_iota(jnp.int32, (1, na), 1)
    eye = lax.broadcasted_iota(jnp.int32, (nr, nr), 0) == lax.broadcasted_iota(
        jnp.int32, (nr, nr), 1
    )
    for q in range(nr):
        one_hot[pl.ds(q, 1), :] = jnp.where(row_lanes == row_map[0, q], 1.0, 0.0)
    loads[4].wait()
    for t in range(nt):
        line = jnp.broadcast_to(weights[0, pl.ds(t, 1), :], (nr, nr))
        column = jnp.sum(jnp.where(eye, line, 0.0), axis=1, keepdims=True)
        face_weight[t] = jnp.where(at_face, column, 0.0)

    loads[0].wait()
    loads[1].wait()

    def pack(t, sums):
        result = []
        for f in range(nf):
            value = field[0, f, t + 1]
            band_out[0, 0, f, pl.ds(t, 1), :] = value[:1]
            band_out[0, 1, f, pl.ds(t, 1), :] = value[nr - 1 :]
            result.append(sums[f] + face_weight[t] * value)
        coef_top[pl.ds(t, 1), :] = coef[1, t + 1, pl.ds(nr - 1, 1), :]
        return tuple(result)

    def halo_copies(k):
        theta_copies = [
            remote(field.at[k, :, nt], theta_in.at[k, 0], send_sem.at[k, 0],
                   recv_sem.at[k, 0], theta=next_theta),
            remote(field.at[k, :, 1], theta_in.at[k, 1], send_sem.at[k, 1],
                   recv_sem.at[k, 1], theta=prev_theta),
        ]
        up = remote(band_out.at[k, 1], band_in.at[k, 0], send_sem.at[k, 2],
                    recv_sem.at[k, 2], band=band + 1)
        down = remote(band_out.at[k, 0], band_in.at[k, 1], send_sem.at[k, 3],
                      recv_sem.at[k, 3], band=band - 1)
        return theta_copies, up, down

    def mix_copies(k, start):
        slot = theta * n_band + band

        def one(i, carry):
            to = lax.rem(slot + i + n_theta * n_band // 2, n_theta * n_band)
            remote(mix_out.at[k], mix_in.at[k, slot], mix_send.at[k], mix_recv.at[k],
                   theta=to // n_band, band=lax.rem(to, n_band), row=1 - row).start()
            return carry

        lax.fori_loop(0, n_theta * n_band, one, 0)

    def send_mix(k, sums):
        hot = one_hot[...]
        for f in range(nf):
            column = jnp.sum(sums[f], axis=1, keepdims=True)
            mix_out[k, pl.ds(f, 1), :] = jnp.sum(hot * column, axis=0, keepdims=True)
        mix_copies(k, True)

    def start_theta(k):
        ahead, behind = halo_copies(k)[0]
        pl.when(theta == 0)(behind.start)
        ahead.start()
        pl.when(theta > 0)(behind.start)

    def start_band(k):
        _, up, down = halo_copies(k)
        pl.when(has_above)(up.start)
        pl.when(has_below)(down.start)

    zero_sums = tuple(jnp.zeros((nr, na), F32) for _ in range(nf))
    for k in range(ITERS):
        mix_out[k] = jnp.zeros((8, na), F32)
    pl.semaphore_wait(barrier, group - 1)
    coef_up = remote(coef_top, coef_band, coef_send.at[1], coef_recv.at[1], band=band + 1)
    coef_next = remote(coef.at[0, nt], coef_theta, coef_send.at[0], coef_recv.at[0],
                       theta=next_theta)
    sums = lax.fori_loop(0, nt, pack, zero_sums, unroll=4)
    send_mix(0, sums)
    start_theta(0)
    start_band(0)
    coef_next.start()
    pl.when(has_above)(coef_up.start)
    loads[2].wait()
    loads[3].wait()
    loads[5].wait()

    chunk_lanes = lax.broadcasted_iota(jnp.int32, (STEP, nr, na), 2)
    chunk_rows = lax.broadcasted_iota(jnp.int32, (STEP, nr, na), 1)

    def lane_up(v):
        return jnp.where(chunk_lanes == na - 1, 0.0, pltpu.roll(v, na - 1, 2))

    def lane_down(v):
        return jnp.where(chunk_lanes == 0, 0.0, pltpu.roll(v, 1, 2))

    def row_up(v):
        return jnp.where(chunk_rows == nr - 1, 0.0, pltpu.roll(v, nr - 1, 1))

    def row_down(v):
        return jnp.where(chunk_rows == 0, 0.0, pltpu.roll(v, 1, 1))

    for k in range(ITERS):

        def bulk(i, carry):
            t = i * STEP
            own = pl.ds(t + 1, STEP)
            total = [-grad[f, pl.ds(t, STEP)] for f in range(nf)]
            c_axial = coef[2, own]
            w = []
            for f in range(nf):
                v = field[k, f, own]
                w.append(c_axial * (v - lane_up(v)))
            total = add_block(total, jac, 2, 0, w)
            total = add_block(total, jac, 2, 1, [lane_down(x) for x in w])
            c_radial = coef[1, own]
            w = []
            for f in range(nf):
                v = field[k, f, own]
                w.append(c_radial * (v - row_up(v)))
            total = add_block(total, jac, 1, 0, w)
            total = add_block(total, jac, 1, 1, [row_down(x) for x in w])
            c_theta = coef[0, pl.ds(t, STEP + 1)]
            w = []
            for f in range(nf):
                v = field[k, f, pl.ds(t, STEP + 2)]
                w.append(c_theta * (v[: STEP + 1] - v[1:]))
            total = add_block(total, jac, 0, 0, [x[1:] for x in w])
            total = add_block(total, jac, 0, 1, [x[:STEP] for x in w])
            for f in range(nf):
                acc[f, pl.ds(t, STEP)] = total[f]
            if k == 0:
                low = row_down(c_radial) + lane_down(c_axial)
                scale[pl.ds(t, STEP)] = (
                    scale[pl.ds(t, STEP)] + c_theta[1:] + c_theta[:STEP] + c_radial + c_axial + low
                )
            return carry

        lax.fori_loop(0, nt // STEP, bulk, 0)

        theta_copies, up, down = halo_copies(k)
        pltpu.make_async_copy(mix_in.at[k], mix_in.at[k], mix_recv.at[k]).wait()
        pltpu.make_async_copy(mix_in.at[k], mix_in.at[k], mix_send.at[k]).wait()
        matched = lax.fori_loop(
            1, n_theta * n_band, lambda i, m: m + mix_in[k, i], mix_in[k, 0]
        )
        here = lanes == rows + band * nr
        for f in range(nf):
            line = mix_jac[0, 0, f] * matched[:1]
            for g in range(1, nf):
                line = line + mix_jac[g, 0, f] * matched[g : g + 1]
            column = jnp.sum(jnp.where(here, line, 0.0), axis=1, keepdims=True)
            plane[f] = jnp.where(at_face, column, 0.0)

        @pl.when(has_above)
        def _():
            up.wait_send()
            down.wait_recv()

        @pl.when(has_below)
        def _():
            down.wait_send()
            up.wait_recv()

        if k == 0:

            @pl.when(has_above)
            def _():
                coef_up.wait_send()

            @pl.when(has_below)
            def _():
                coef_up.wait_recv()

        flat = jnp.zeros((nt, na), F32)
        below = [coef_band[...] * (band_in[k, 0, f] - band_out[k, 0, f]) for f in range(nf)]
        total = add_block([flat] * nf, jac, 1, 1, below)
        above = [coef_top[...] * band_in[k, 1, f] for f in range(nf)]
        other = add_block([flat] * nf, jac, 1, 0, above, -1.0)
        for f in range(nf):
            corr[0, f] = total[f]
            corr[1, f] = other[f]

        for copy in theta_copies:
            copy.wait()
        if k == 0:
            coef_next.wait()

            scale[0] += coef_theta[...]
        before = [coef_theta[...] * (theta_in[k, 0, f] - field[k, f, 1]) for f in range(nf)]
        total = add_block([acc[f, 0] for f in range(nf)], jac, 0, 1, before)
        for f in range(nf):
            acc[f, 0] = total[f]
        after = [coef[0, nt] * theta_in[k, 1, f] for f in range(nf)]
        total = add_block([acc[f, nt - 1] for f in range(nf)], jac, 0, 0, after, -1.0)
        for f in range(nf):
            acc[f, nt - 1] = total[f]

        def finish(t, sums):
            if k == 0:
                bottom = jnp.where(rows == 0, coef_band[pl.ds(t, 1), :], 0.0)
                gain = OMEGA / (scale[t] + bottom)
                scale[t] = gain
            else:
                gain = scale[t]
            result = []
            for f in range(nf):
                resid = acc[f, t] + plane[f]
                resid = resid + jnp.where(rows == 0, corr[0, f, pl.ds(t, 1), :], 0.0)
                resid = resid + jnp.where(rows == nr - 1, corr[1, f, pl.ds(t, 1), :], 0.0)
                value = field[k, f, t + 1] - gain * resid
                if k < ITERS - 1:
                    field[k + 1, f, t + 1] = value
                    band_out[k + 1, 0, f, pl.ds(t, 1), :] = value[:1]
                    band_out[k + 1, 1, f, pl.ds(t, 1), :] = value[nr - 1 :]
                    result.append(sums[f] + face_weight[t] * value)
                else:
                    out[0, f, t] = value
            return tuple(result) if k < ITERS - 1 else sums

        if k < ITERS - 1:
            sums = lax.fori_loop(0, nt, finish, zero_sums, unroll=4)
            send_mix(k + 1, sums)
            start_band(k + 1)
            start_theta(k + 1)
        else:
            finish(0, 0)
            weighted = surf[0, 0, 0] * out[0, 0, 0]
            for f in range(1, nf):
                weighted = weighted + surf[0, f, 0] * out[0, f, 0]
            tile_rows = lax.broadcasted_iota(jnp.int32, (8, na), 0)

            owners = 8 // own_modes

            def part(d, carry):
                mode = tile_rows + d * 8
                total = jnp.zeros((8, na), F32)
                for r in range(nr):
                    total = total + jnp.where(mode == modes[0, 0, r], weighted[r : r + 1], 0.0)
                for j in range(owners):
                    sens_part[d * owners + j] = total[j * own_modes : (j + 1) * own_modes]
                return carry

            lax.fori_loop(0, group // owners, part, 0, unroll=2)

            def send(i, carry):
                to = lax.rem(me + i, group)
                remote(sens_part.at[to], sens_in.at[i - 1], sens_send.at[0], sens_recv.at[0],
                       **device(to)).start()
                return carry

            lax.fori_loop(1, group, send, 0)
            lax.fori_loop(1, nt, finish, 0, unroll=3)
            pltpu.make_async_copy(sens_in, sens_in, sens_recv.at[0]).wait()
            pltpu.make_async_copy(sens_in, sens_in, sens_send.at[0]).wait()
            total = lax.fori_loop(0, group - 1, lambda i, s: s + sens_in[i], sens_part[me])
            sens_out[...] = total


def local(sizes, *args):
    adjoint = args[0]
    n_theta, n_band, own_modes = sizes
    _, nf, nt, nr, na = adjoint.shape
    group = n_theta * n_band * 2
    dma = pltpu.SemaphoreType.DMA
    hbm = pl.BlockSpec(memory_space=pltpu.HBM)
    vmem = pl.BlockSpec(memory_space=pltpu.VMEM)
    smem = pl.BlockSpec(memory_space=pltpu.SMEM)
    return pl.pallas_call(
        functools.partial(kernel, (n_theta, n_band, nf, nt, nr, na, own_modes)),
        out_shape=(
            pltpu.VMEM(adjoint.shape, F32),
            pltpu.VMEM((own_modes, na), F32),
        ),
        in_specs=[hbm] * 4 + [smem, hbm, smem, smem, hbm, smem],
        out_specs=(vmem, vmem),
        scratch_shapes=[
            pltpu.VMEM((ITERS, nf, nt + 2, nr, na), F32),
            pltpu.VMEM((3, nt + 1, nr, na), F32),
            pltpu.VMEM((nf, nt, nr, na), F32),
            pltpu.VMEM((nt, nr, na), F32),
            pltpu.VMEM((nf, nt, nr, na), F32),
            pltpu.VMEM((ITERS, 2, nf, nr, na), F32),
            pltpu.VMEM((ITERS, 2, nf, nt, na), F32),
            pltpu.VMEM((ITERS, 2, nf, nt, na), F32),
            pltpu.VMEM((nr, na), F32),
            pltpu.VMEM((nt, na), F32),
            pltpu.VMEM((nt, na), F32),
            pltpu.VMEM((nt, nr, na), F32),
            pltpu.VMEM((nr, na), F32),
            pltpu.VMEM((2, nf, nt, na), F32),
            pltpu.VMEM((nf, nr, na), F32),
            pltpu.VMEM((ITERS, 8, na), F32),
            pltpu.VMEM((ITERS, n_theta * n_band, 8, na), F32),
            pltpu.VMEM((group, own_modes, na), F32),
            pltpu.VMEM((group - 1, own_modes, na), F32),
            pltpu.VMEM((1, nt, nr), F32),
            pltpu.VMEM((1, nf, 1, nr, na), F32),
            dma((6,)),
            dma((ITERS, 4)),
            dma((ITERS, 4)),
            dma((2,)),
            dma((2,)),
            dma((ITERS,)),
            dma((ITERS,)),
            dma((1,)),
            dma((1,)),
        ],
        compiler_params=pltpu.CompilerParams(
            collective_id=0, has_side_effects=True, vmem_limit_bytes=63 * 1024 * 1024
        ),
    )(*args[:4], jnp.swapaxes(args[4], 2, 3), *args[5:7], jnp.swapaxes(args[7], 0, 1), *args[8:])


def solution(mesh):
    cells = P(("samples", "row"), None, "theta", "band", None)
    placed = (
        cells,
        cells,
        cells,
        P(("samples", "row"), "theta", "band", None),
        P("row", None, None, None, None),
        P(("samples", "row"), "theta", "band"),
        P(("samples", "row"), "band"),
        P("row", None, None),
        cells,
        P(("samples", "row"), "theta", "band"),
    )
    return jax.shard_map(
        functools.partial(local, (mesh.shape["theta"], mesh.shape["band"], 2)),
        mesh=mesh,
        in_specs=placed,
        out_specs=(cells, P(("samples", "theta", "band", "row"), None)),
        check_vma=False,
    )
```
